32 devices in a mesh: section: 1, expert: 32 (over z, y, x, core).
Axes of the slice: x: 2, y: 2, z: 4, core: 2. Of those that a mesh axis runs over, the one named last changes fastest.
Arguments:
- acts: bfloat16 [1, 2, 2048, 3584], P('section', None, 'expert'), may hold values from -6 to 6
- norm_gain: float32 [1, 3584], P('section'), may hold values from 0.1 to 1.9
- router: bfloat16 [1, 3584, 8], P('section'), may hold values from -0.09375 to 0.09375
- routes: int32 [1, 2, 2, 2048, 1], P('section', None, None, 'expert'), may hold values from 0 to 7; in each aligned block of 64 rows (0 to 63, 64 to 127, ..., all dimensions but the last counted through in order) at most 16 rows name the same one
- w_gate: bfloat16 [1, 32, 3584, 256], P('section', 'expert'), may hold values from -0.09375 to 0.09375
- w_up: bfloat16 [1, 32, 3584, 256], P('section', 'expert'), may hold values from -0.09375 to 0.09375
- w_down: bfloat16 [1, 32, 256, 3584], P('section', 'expert'), may hold values from -0.375 to 0.375
Outputs:
- finished: bfloat16 [1, 2, 2048, 3584], P('section', None, 'expert')
The draws below stay inside these ranges and needn't reach their ends.
Inputs may be any that keep to these rules, and one draw needn't show every extreme that they name: `routes`: within each block of 64 tokens of one device, for each layer, round and micro-batch, no expert is named by more than 16 tokens, a bound that some block reaches.
All inputs are finite; a program needn't handle non-finite values.
Results may differ from the reference program's by a relative error of at most 0.0072.
Values may be sent and summed in bfloat16 or wider, within the bound.
A program may use at most 128 MiB of HBM per device.

```python
import math
import jax
import jax.numpy as jnp
import numpy as np
from jax import lax

D = 3584
GRP = 4
HID = 256
NEXP = 8
TOK_DEV = 64
MB = 2
ROUNDS = 2
CAP = 16
TOKENS = 2048
N_SECTION = 1
N_EXPERT = 32


def shard_levels(stream_key, dims, split, smallest, high):
    loudness, own = 1.0, jax.random.fold_in(stream_key, 6)
    for dim, shards_of in split:
        heights = jnp.exp(jax.random.uniform(jax.random.fold_in(own, dim), (shards_of,), jnp.float32, smallest / len(split), high / len(split)))
        loudness = loudness * jnp.repeat(heights, dims[dim] // shards_of).reshape([-1 if axis == dim else 1 for axis in range(len(dims))])
    return loudness


def shared_out(own_key, own, number, rows, count, top, most, lean):
    sequence = jax.random.permutation(own_key, count)
    crowded, common = portions_of(count, rows * top, most, lean, True), portions_of(count, rows * top, most, lean, False)
    places = jnp.arange(count)

    def named(lengths, turn):
        used = int((lengths > 0).sum())
        fixed = max(1, used // 4)
        moved = fixed + (places - fixed + turn * (used - fixed)) % max(1, count - fixed)
        return jnp.zeros((count,), jnp.int32).at[sequence[jnp.where(places < fixed, places, moved)]].set(jnp.asarray(lengths, jnp.int32))

    lengths = jnp.where(number % 4 == 0, named(crowded, number // 4), named(common, number - number // 4 - 1))
    mixed = jax.random.permutation(jax.random.fold_in(own, 3), count)
    donor, taker = mixed[0:count // 2 * 2:2], mixed[1:count // 2 * 2:2]
    margin = jnp.minimum(lengths[donor] - 1, most - lengths[taker]) // 2
    margin = jnp.where((donor == sequence[0]) | (taker == sequence[0]) | (lengths[taker] == 0), 0, jnp.maximum(margin, 0))
    moved = jax.random.randint(jax.random.fold_in(own, 4), (count // 2,), 0, 1 << 20) % (margin + 1)
    lengths = lengths.at[donor].add(-moved).at[taker].add(moved)
    members = jnp.searchsorted(jnp.cumsum(lengths), jnp.arange(rows * top), side="right").astype(jnp.int32)
    table = members.reshape(top, rows).T
    table = table[jax.random.permutation(jax.random.fold_in(own, 1), rows)]
    turn = jax.random.randint(jax.random.fold_in(own, 2), (rows, 1), 0, top)
    return jnp.take_along_axis(table, (jnp.arange(top)[None, :] + turn) % top, axis=1)


def portions_of(number_of, total, limit, skew, full):
    weights = [(1 << 20) // math.isqrt(rank ** skew) + 1 for rank in range(1, number_of + 1)]
    largest = limit if full else min(limit, max(-(-total // number_of), total * weights[0] // sum(weights)))
    least = 1 if total - largest >= number_of - 1 else 0
    holding, spare = [largest] + [least] * (number_of - 1), total - largest - least * (number_of - 1)
    while spare > 0:
        candidates = [i for i in range(1, number_of) if holding[i] < largest] or [i for i in range(1, number_of) if holding[i] < limit]
        pool, remaining = sum([weights[i] for i in candidates]), spare
        for i in candidates:
            extra = min(limit - holding[i], max(1, remaining * weights[i] // pool), spare)
            holding[i] = holding[i] + extra
            spare = spare - extra
    return np.array(holding)


def noise(own_key, shape, width, limit, cuts=(), held_as=jnp.bfloat16):
    factor_of = shard_levels(own_key, shape, cuts, -0.22, 0.18) if cuts else 1.0
    array = jax.random.normal(own_key, shape, jnp.float32) * width * factor_of
    return jnp.minimum(jnp.maximum(array, -limit), limit).astype(held_as)


def setup_inputs(seed: int = 0) -> dict:
    splits = jax.random.split(jax.random.key(seed), 8)
    acts = noise(splits[0], (N_SECTION, MB, TOKENS, D), 1.0, 6.0, ((2, 32),))
    norm_gain = jnp.clip(1.0 + 0.18 * jax.random.normal(splits[1], (N_SECTION, D), jnp.float32), 0.1, 1.9)
    router = noise(splits[2], (N_SECTION, D, NEXP), D ** -0.5, 0.09375)
    routes_keys = jax.random.split(jax.random.fold_in(splits[3], 1), N_SECTION * ROUNDS * MB * TOKENS // TOK_DEV)
    routes_turns = jax.random.permutation(jax.random.fold_in(splits[3], 3), N_SECTION * ROUNDS * MB * TOKENS // TOK_DEV)
    routes = jax.vmap(lambda own, number: shared_out(jax.random.fold_in(splits[3], 2), own, number, TOK_DEV, NEXP, 1, CAP, 2))(routes_keys, routes_turns).reshape((N_SECTION, ROUNDS, MB, TOKENS, 1))
    w_gate = noise(splits[4], (N_SECTION, N_EXPERT, D, HID), D ** -0.5, 0.09375, ((1, 32),))
    w_up = noise(splits[5], (N_SECTION, N_EXPERT, D, HID), D ** -0.5, 0.09375, ((1, 32),))
    w_down = noise(splits[6], (N_SECTION, N_EXPERT, HID, D), HID ** -0.5, 0.375, ((1, 32),))
    return {"acts": acts, "norm_gain": norm_gain, "router": router, "routes": routes, "w_gate": w_gate, "w_up": w_up, "w_down": w_down}


def run_layer(tokens_in, route_ids, gain_row, router_mat, gate_blocks, up_blocks, down_blocks):
    x_float = tokens_in.astype(jnp.float32)
    mean_sq = lax.optimization_barrier(jnp.mean(x_float * x_float, axis=1, keepdims=True))
    normed = (x_float * lax.rsqrt(mean_sq + 1e-06) * gain_row[None, :]).astype(jnp.bfloat16)
    scores = jnp.dot(normed, router_mat, preferred_element_type=jnp.float32)
    chosen = route_ids[:, 0].astype(jnp.int32)
    onehot = (chosen[:, None] == jnp.arange(NEXP, dtype=jnp.int32)[None, :]).astype(jnp.int32)
    gate_val = jax.nn.sigmoid(lax.optimization_barrier(jnp.sum(scores * onehot.astype(jnp.float32), axis=1)))
    per_block = onehot.reshape(N_EXPERT, TOK_DEV, NEXP)
    slot_of = (lax.optimization_barrier(jnp.sum(jnp.cumsum(per_block, axis=1) * per_block, axis=2)) - 1).reshape(TOKENS).astype(jnp.int32)
    source = jnp.repeat(jnp.arange(N_EXPERT, dtype=jnp.int32), TOK_DEV)
    outbox = jnp.zeros((NEXP, N_EXPERT, CAP, D), jnp.bfloat16).at[chosen, source, slot_of].set(normed)
    gate_sorted = jnp.transpose(gate_blocks.reshape(GRP, NEXP, D, HID), (1, 0, 2, 3))
    up_sorted = jnp.transpose(up_blocks.reshape(GRP, NEXP, D, HID), (1, 0, 2, 3))
    down_sorted = jnp.transpose(down_blocks.reshape(GRP, NEXP, HID, D), (1, 0, 2, 3))

    def expert_out(packed):
        rows_box, gate_mats, up_mats, down_mats = packed
        rows_in = rows_box.reshape(N_EXPERT * CAP, D)
        total = jnp.zeros((N_EXPERT * CAP, D), jnp.float32)
        for block_idx in range(GRP):
            gate_proj = jnp.dot(rows_in, gate_mats[block_idx], preferred_element_type=jnp.float32)
            up_proj = jnp.dot(rows_in, up_mats[block_idx], preferred_element_type=jnp.float32)
            hidden = (jax.nn.silu(gate_proj) * up_proj).astype(jnp.bfloat16)
            partial_out = jnp.dot(hidden, down_mats[block_idx], preferred_element_type=jnp.float32).astype(jnp.bfloat16)
            total = total + partial_out.astype(jnp.float32)
        return total
    combined = lax.map(expert_out, (outbox, gate_sorted, up_sorted, down_sorted))
    combined = combined.reshape(NEXP, N_EXPERT, CAP, D)
    picked = combined[chosen, source, slot_of]
    return (x_float + gate_val[:, None] * picked).astype(jnp.bfloat16)

def reference(acts, norm_gain, router, routes, w_gate, w_up, w_down):
    carried = [[acts[group_idx, micro_idx] for micro_idx in range(MB)] for group_idx in range(N_SECTION)]
    for round_idx in range(ROUNDS):
        for group_idx in range(N_SECTION):
            section_idx = (group_idx + round_idx) % N_SECTION
            for micro_idx in range(MB):
                carried[group_idx][micro_idx] = run_layer(carried[group_idx][micro_idx], routes[section_idx, round_idx, micro_idx], norm_gain[section_idx], router[section_idx], w_gate[section_idx], w_up[section_idx], w_down[section_idx])
    result = jnp.stack([jnp.stack(row_list) for row_list in carried])
    return jnp.roll(result, ROUNDS, axis=0)
```

```python
import functools

import jax
import jax.numpy as jnp
from jax import lax
from jax.experimental import pallas as pl
from jax.experimental.pallas import tpu as pltpu
from jax.sharding import PartitionSpec as P

MESH = pl.DeviceIdType.MESH


def flipped(value, flips, count):
    total, bit = 0, 1
    while bit < count:
        total = total + bit * (((value // bit) % 2 + (flips // bit) % 2) % 2)
        bit *= 2
    return total


def column_tile(width):
    for tile in (512, 256, 128):
        if width % tile == 0:
            return tile
    return width


def layers_kernel(
    rounds,
    micros,
    planes,
    experts,
    capacity,
    acts_ref,
    gain_ref,
    router_ref,
    route_rows_ref,
    route_cols_ref,
    gate_ref,
    up_ref,
    down_ref,
    out_ref,
    peer_routes,
    tokens,
    outbox,
    inbox,
    partial,
    returned,
    plane_send,
    plane_back,
    route_send_sem,
    route_recv_sem,
    token_send_sem,
    token_recv_sem,
    out_send_sem,
    in_recv_sem,
    part_send_sem,
    ret_recv_sem,
    back_send_sem,
    back_recv_sem,
):
    me = lax.axis_index("expert")
    plane, place = me // experts, me % experts
    tok, width = acts_ref.shape[1], acts_ref.shape[2]
    tile = column_tile(width)
    tiles = width // tile
    slots = experts * capacity

    def cols(c):
        return pl.ds(pl.multiple_of(c * tile, tile), tile)

    def remote(src, dst, send_sem, recv_sem, to):
        return pltpu.make_async_remote_copy(
            src_ref=src,
            dst_ref=dst,
            send_sem=send_sem,
            recv_sem=recv_sem,
            device_id={"expert": to},
            device_id_type=MESH,
        )

    def plane_peer(k):
        return flipped(plane, k, planes)

    def place_peer(d):
        return flipped(place, d, experts)

    def each(first, last, step):
        lax.fori_loop(first, last, lambda i, carry: (step(i), carry)[1], 0)

    barrier = pltpu.get_barrier_semaphore()

    def greet_plane(k):
        to = plane_peer(k) * experts + place
        pl.semaphore_signal(barrier, inc=1, device_id={"expert": to}, device_id_type=MESH)

    def greet_place(d):
        to = plane * experts + place_peer(d)
        pl.semaphore_signal(barrier, inc=1, device_id={"expert": to}, device_id_type=MESH)

    each(1, planes, greet_plane)
    each(1, experts, greet_place)
    pl.semaphore_wait(barrier, planes + experts - 2)

    def route_copy(k, source):
        return remote(
            peer_routes.at[source],
            peer_routes.at[source],
            route_send_sem.at[k],
            route_recv_sem.at[source],
            plane_peer(k) * experts + place,
        )

    def token_copy(m, k, source):
        return remote(
            tokens.at[m, source],
            tokens.at[m, source],
            token_send_sem.at[m, k],
            token_recv_sem.at[m, source],
            plane_peer(k) * experts + place,
        )

    def out_copy(m, q, to, source):
        return remote(
            outbox.at[m, q, to],
            inbox.at[m, q, source],
            out_send_sem.at[m, q, to],
            in_recv_sem.at[m, q, source],
            plane * experts + to,
        )

    def out_local(m, q):
        return pltpu.make_async_copy(
            outbox.at[m, q, place], inbox.at[m, q, place], in_recv_sem.at[m, q, place]
        )

    def part_copy(m, q, to, source):
        return remote(
            partial.at[m, q, to],
            returned.at[m, q, source],
            part_send_sem.at[m, q, to],
            ret_recv_sem.at[m, q, source],
            plane * experts + to,
        )

    def part_local(m, q):
        return pltpu.make_async_copy(
            partial.at[m, q, place], returned.at[m, q, place], ret_recv_sem.at[m, q, place]
        )

    def back_copy(m, q, source):
        return remote(
            plane_send.at[m, q],
            plane_back.at[m, source],
            back_send_sem.at[m, q],
            back_recv_sem.at[m, source],
            q * experts + place,
        )

    def placing_of(r, m, q):
        chosen = peer_routes[q, pl.ds(r * micros + m, 1), :][:, :tok]
        onehot = lax.broadcasted_iota(jnp.int32, (experts, tok), 0) == chosen
        earlier = lax.broadcasted_iota(jnp.int32, (tok, tok), 0) < lax.broadcasted_iota(
            jnp.int32, (tok, tok), 1
        )
        counts = jnp.dot(
            onehot.astype(jnp.float32).astype(jnp.bfloat16),
            earlier.astype(jnp.float32).astype(jnp.bfloat16),
            preferred_element_type=jnp.float32,
        )
        slot = jnp.sum(jnp.where(onehot, counts, 0.0), axis=0, keepdims=True).astype(jnp.int32)
        flat = chosen * capacity + slot
        return (lax.broadcasted_iota(jnp.int32, (slots, tok), 0) == flat).astype(jnp.float32)

    def norm_and_send(r, m):
        source = acts_ref if r == 0 else out_ref
        if r > 0:
            each(1, planes, lambda k: token_copy(m, k, plane).wait_send())

        def add_squares(c, total):
            x = source[m, :, cols(c)].astype(jnp.float32)
            return total + jnp.sum(x * x, axis=1, keepdims=True)

        squares = lax.fori_loop(0, tiles, add_squares, jnp.zeros((tok, 1), jnp.float32))
        scale = lax.rsqrt(squares / width + 1e-06)

        def scaled(c):
            x = source[m, :, cols(c)].astype(jnp.float32)
            tokens[m, plane, :, cols(c)] = (x * scale * gain_ref[:, cols(c)]).astype(jnp.bfloat16)

        each(0, tiles, scaled)
        each(1, planes, lambda k: token_copy(m, k, plane).start())
        scores = jnp.dot(tokens[m, plane], router_ref[...], preferred_element_type=jnp.float32)
        chosen = route_cols_ref[r, m]
        onehot = lax.broadcasted_iota(jnp.int32, (tok, experts), 1) == chosen
        return jax.nn.sigmoid(jnp.sum(jnp.where(onehot, scores, 0.0), axis=1, keepdims=True))

    def pack(r, m, k):
        q = plane_peer(k)

        @pl.when(k > 0)
        def _():
            token_copy(m, k, q).wait_recv()

        if r > 0:
            each(1, experts, lambda d: out_copy(m, q, place_peer(d), place).wait_send())
        placing = placing_of(r, m, q).astype(jnp.bfloat16)

        def packed(c):
            rows = jnp.dot(placing, tokens[m, q, :, cols(c)], preferred_element_type=jnp.float32)
            outbox[m, q, :, :, cols(c)] = rows.astype(jnp.bfloat16).reshape(
                experts, capacity, tile
            )

        each(0, tiles, packed)
        out_local(m, q).start()
        each(1, experts, lambda d: out_copy(m, q, place_peer(d), place).start())

    def expert(r, m, k):
        q = plane_peer(k)
        out_local(m, q).wait()

        def arrived(d):
            out_copy(m, q, place_peer(d), place_peer(d)).wait_recv()

        each(1, experts, arrived)
        if r > 0:
            each(1, experts, lambda d: part_copy(m, q, place_peer(d), place).wait_send())
        rows = inbox[m, q].reshape(slots, width)
        gate_proj = jnp.dot(rows, gate_ref[...], preferred_element_type=jnp.float32)
        up_proj = jnp.dot(rows, up_ref[...], preferred_element_type=jnp.float32)
        hidden = (jax.nn.silu(gate_proj) * up_proj).astype(jnp.bfloat16)

        def projected(c):
            part = jnp.dot(hidden, down_ref[:, cols(c)], preferred_element_type=jnp.float32)
            partial[m, q, :, :, cols(c)] = part.astype(jnp.bfloat16).reshape(
                experts, capacity, tile
            )

        each(0, tiles, projected)
        part_local(m, q).start()
        each(1, experts, lambda d: part_copy(m, q, place_peer(d), place).start())

    def unpack(r, m, k):
        q = plane_peer(k)
        part_local(m, q).wait()

        def arrived(d):
            part_copy(m, q, place_peer(d), place_peer(d)).wait_recv()

        each(1, experts, arrived)
        if r > 0:

            @pl.when(k > 0)
            def _():
                back_copy(m, q, plane).wait_send()

        picking = placing_of(r, m, q).T.astype(jnp.bfloat16)

        def picked(c):
            rows = returned[m, q, :, :, cols(c)].reshape(slots, tile)
            plane_send[m, q, :, cols(c)] = jnp.dot(
                picking, rows, preferred_element_type=jnp.float32
            ).astype(jnp.bfloat16)

        each(0, tiles, picked)

        @pl.when(k > 0)
        def _():
            back_copy(m, q, plane).start()

    def finish(r, m, gate_val):
        source = acts_ref if r == 0 else out_ref
        each(1, planes, lambda k: back_copy(m, plane_peer(k), plane_peer(k)).wait_recv())

        def summed(c):
            total = plane_send[m, plane, :, cols(c)].astype(jnp.float32)
            for k in range(1, planes):
                total += plane_back[m, plane_peer(k), :, cols(c)].astype(jnp.float32)
            x = source[m, :, cols(c)].astype(jnp.float32)
            out_ref[m, :, cols(c)] = (x + gate_val * total).astype(jnp.bfloat16)

        each(0, tiles, summed)

    def steps(phase, r, m):
        each(0, planes, lambda k: phase(r, m, k))

    peer_routes[plane] = route_rows_ref[...]
    each(1, planes, lambda k: route_copy(k, plane).start())
    gates = {}
    gates[0] = norm_and_send(0, 0)
    each(1, planes, lambda k: route_copy(k, plane_peer(k)).wait_recv())
    steps(pack, 0, 0)
    for r in range(rounds):
        for m in range(micros):
            after = m + 1 if m + 1 < micros else 0
            after_round = r if m + 1 < micros else r + 1
            if m + 1 < micros:
                if r == 0:
                    gates[after] = norm_and_send(r, after)
                steps(expert, r, m)
                steps(pack, r, after)
            else:
                ahead = after_round < rounds and micros > 1
                if ahead:
                    steps(unpack, r, 0)
                    finish(r, 0, gates[0])
                    gates[0] = norm_and_send(r + 1, 0)
                steps(expert, r, m)
                if ahead:
                    steps(pack, r + 1, 0)
                for other in range(1 if ahead else 0, micros):
                    steps(unpack, r, other)
                    finish(r, other, gates[other])
                    if r + 1 < rounds and other > 0:
                        gates[other] = norm_and_send(r + 1, other)
                if r + 1 < rounds and micros == 1:
                    gates[0] = norm_and_send(r + 1, 0)
                    steps(pack, r + 1, 0)

    each(1, planes, lambda k: route_copy(k, plane).wait_send())
    for m in range(micros):
        each(1, planes, lambda k: token_copy(m, k, plane).wait_send())

        def sent(k):
            q = plane_peer(k)
            each(1, experts, lambda d: out_copy(m, q, place_peer(d), place).wait_send())
            each(1, experts, lambda d: part_copy(m, q, place_peer(d), place).wait_send())

            @pl.when(k > 0)
            def _():
                back_copy(m, q, plane).wait_send()

        each(0, planes, sent)


def run_layers(acts, gain, router, routes, gate_mat, up_mat, down_mat):
    devices = lax.axis_size("expert")
    experts = router.shape[1]
    planes = devices // experts
    micros, tok, width = acts.shape
    rounds = routes.shape[0]
    capacity = 2 * tok // experts
    hidden = gate_mat.shape[1]
    rows = rounds * micros
    row_pad, lane_pad = -(-rows // 8) * 8, -(-tok // 128) * 128
    route_rows = jnp.pad(
        routes.reshape(rows, tok), ((0, row_pad - rows), (0, lane_pad - tok))
    )
    vmem = pl.BlockSpec(memory_space=pltpu.VMEM)
    dma = pltpu.SemaphoreType.DMA
    slot_shape = (micros, planes, experts, capacity, width)
    plane_shape = (micros, planes, tok, width)
    slots = experts * capacity
    flops = 2 * rows * planes * slots * width * hidden * 3
    return pl.pallas_call(
        functools.partial(layers_kernel, rounds, micros, planes, experts, capacity),
        out_shape=jax.ShapeDtypeStruct(acts.shape, acts.dtype),
        in_specs=[vmem] * 8,
        out_specs=vmem,
        scratch_shapes=[
            pltpu.VMEM((planes, row_pad, lane_pad), jnp.int32),
            pltpu.VMEM(plane_shape, jnp.bfloat16),
            pltpu.VMEM(slot_shape, jnp.bfloat16),
            pltpu.VMEM(slot_shape, jnp.bfloat16),
            pltpu.VMEM(slot_shape, jnp.bfloat16),
            pltpu.VMEM(slot_shape, jnp.bfloat16),
            pltpu.VMEM(plane_shape, jnp.bfloat16),
            pltpu.VMEM(plane_shape, jnp.bfloat16),
            dma((planes,)),
            dma((planes,)),
            dma((micros, planes)),
            dma((micros, planes)),
            dma((micros, planes, experts)),
            dma((micros, planes, experts)),
            dma((micros, planes, experts)),
            dma((micros, planes, experts)),
            dma((micros, planes)),
            dma((micros, planes)),
        ],
        compiler_params=pltpu.CompilerParams(
            collective_id=0, has_side_effects=True, vmem_limit_bytes=62 * 1024 * 1024
        ),
        cost_estimate=pl.CostEstimate(
            flops=flops,
            bytes_accessed=3 * gate_mat.size * 2 + 4 * acts.size,
            transcendentals=rows * planes * slots * hidden,
        ),
    )(acts, gain, router, route_rows, routes, gate_mat, up_mat, down_mat)


def body(acts, norm_gain, router, routes, w_gate, w_up, w_down):
    sections = lax.axis_size("section")
    rounds = routes.shape[1]
    weights = (w_gate[0, 0], w_up[0, 0], w_down[0, 0])
    if sections == 1:
        return run_layers(acts[0], norm_gain, router[0], routes[0], *weights)[None]
    carried = acts[0]
    pairs = [(source, (source + 1) % sections) for source in range(sections)]
    for r in range(rounds):
        carried = run_layers(carried, norm_gain, router[0], routes[0, r : r + 1], *weights)
        carried = lax.ppermute(carried, "section", pairs)
    return carried[None]


def solution(mesh):
    in_specs = (
        P("section", None, "expert", None),
        P("section", None),
        P("section", None, None),
        P("section", None, None, "expert", None),
        P("section", "expert", None, None),
        P("section", "expert", None, None),
        P("section", "expert", None, None),
    )
    out_specs = P("section", None, "expert", None)
    return jax.shard_map(body, mesh=mesh, in_specs=in_specs, out_specs=out_specs, check_vma=False)
```

```python
import functools

import jax
import jax.numpy as jnp
from jax import lax
from jax.experimental import pallas as pl
from jax.experimental.pallas import tpu as pltpu
from jax.sharding import PartitionSpec as P

MESH = pl.DeviceIdType.MESH


def flipped(value, flips, count):
    total, bit = 0, 1
    while bit < count:
        total = total + bit * (((value // bit) % 2 + (flips // bit) % 2) % 2)
        bit *= 2
    return total


def at_least(a, b):
    return (a - b + (1 << 16)) // (1 << 16)


def nearest(plane, j, planes):
    above_is_more = at_least(planes - 1 - plane, plane + 1)
    paired = above_is_more * plane + (1 - above_is_more) * (planes - 1 - plane)
    in_pairs = at_least(2 * paired, j)
    of_pair = (j + 1) // 2 * (1 - 2 * (j % 2))
    beyond = (j - paired) * (2 * above_is_more - 1)
    return plane + in_pairs * of_pair + (1 - in_pairs) * beyond


def column_tile(width):
    for tile in (512, 256, 128):
        if width % tile == 0:
            return tile
    return width


def order_of_work(rounds, micros, planes):
    work = [(r, m) for r in range(rounds) for m in range(micros)]
    stages = {}
    for r, m in work:
        stages[r, m] = {
            kind: [(kind, r, m, k) for k in range(planes)] for kind in ("pack", "expert", "unpack")
        }
    order = [("norm", 0, 0, 0), ("routes", 0, 0, 0)]
    left = []
    for at, (r, m) in enumerate(work):
        mine = stages[r, m]
        packs, experts = mine["pack"], mine["expert"]
        if at == 0:
            order += packs[:2]
            for k in range(2, planes):
                order += [experts[k - 2], packs[k]]
            done = planes - 2
        else:
            rest = packs[1:]
            while rest or left:
                order += rest[:1]
                rest = rest[1:]
                order += left[:1]
                left = left[1:]
                if not rest and len(left) == 2:
                    break
            done = 0
            before = work[at - 1]
            while left:
                order += [experts[done], left[0]]
                left = left[1:]
                done += 1
            order += [experts[done]]
            done += 1
            order += [("finish", before[0], before[1], 0)]
        if at + 1 < len(work):
            nxt = work[at + 1]
            if micros == 1:
                order += experts[done:] + mine["unpack"] + [("finish", r, m, 0)]
                order += [("norm", nxt[0], nxt[1], 0), stages[nxt]["pack"][0]]
                left, done = [], planes
            else:
                order += [("norm", nxt[0], nxt[1], 0), stages[nxt]["pack"][0]]
                left = experts[done:] + mine["unpack"]
        else:
            order += experts[done:] + mine["unpack"] + [("finish", r, m, 0)]
    return order


def layers_kernel(
    rounds,
    micros,
    planes,
    experts,
    capacity,
    acts_ref,
    gain_ref,
    router_ref,
    route_rows_ref,
    route_cols_ref,
    gate_ref,
    up_ref,
    down_ref,
    out_ref,
    peer_routes,
    tokens,
    outbox,
    inbox,
    partial,
    returned,
    plane_send,
    plane_back,
    route_send_sem,
    route_recv_sem,
    token_send_sem,
    token_recv_sem,
    out_send_sem,
    in_recv_sem,
    part_send_sem,
    ret_recv_sem,
    back_send_sem,
    back_recv_sem,
):
    me = lax.axis_index("expert")
    plane, place = me // experts, me % experts
    tok, width = acts_ref.shape[1], acts_ref.shape[2]
    tile = column_tile(width)
    tiles = width // tile
    slots = experts * capacity

    def cols(c):
        return pl.ds(pl.multiple_of(c * tile, tile), tile)

    def remote(src, dst, send_sem, recv_sem, to):
        return pltpu.make_async_remote_copy(
            src_ref=src,
            dst_ref=dst,
            send_sem=send_sem,
            recv_sem=recv_sem,
            device_id={"expert": to},
            device_id_type=MESH,
        )

    def plane_peer(k):
        return flipped(plane, k, planes)

    def place_peer(d):
        return flipped(place, d, experts)

    def each(first, last, step):
        lax.fori_loop(first, last, lambda i, carry: (step(i), carry)[1], 0)

    barrier = pltpu.get_barrier_semaphore()

    def greet_plane(k):
        to = plane_peer(k) * experts + place
        pl.semaphore_signal(barrier, inc=1, device_id={"expert": to}, device_id_type=MESH)

    def greet_place(d):
        to = plane * experts + place_peer(d)
        pl.semaphore_signal(barrier, inc=1, device_id={"expert": to}, device_id_type=MESH)

    each(1, planes, greet_plane)
    each(1, experts, greet_place)
    pl.semaphore_wait(barrier, planes + experts - 2)

    def route_copy(k, source):
        return remote(
            peer_routes.at[source],
            peer_routes.at[source],
            route_send_sem.at[k],
            route_recv_sem.at[source],
            plane_peer(k) * experts + place,
        )

    def token_copy(m, source, step):
        slot = source if step == 1 else source + at_least(source, plane) * at_least(plane, source) * (
            planes - source
        )
        return remote(
            tokens.at[m, source],
            tokens.at[m, source],
            token_send_sem.at[m, slot],
            token_recv_sem.at[m, source],
            (me + (step + planes) * experts) % (planes * experts),
        )

    def passing(m, q, act):
        @pl.when(jnp.logical_and(q <= plane, plane < planes - 1))
        def _():
            act(token_copy(m, q, 1))

        @pl.when(jnp.logical_and(q >= plane, plane > 0))
        def _():
            act(token_copy(m, q, -1))

    def out_copy(m, q, to, source):
        return remote(
            outbox.at[m, q, to],
            inbox.at[m, q, source],
            out_send_sem.at[m, q, to],
            in_recv_sem.at[m, q, source],
            plane * experts + to,
        )

    def out_local(m, q):
        return pltpu.make_async_copy(
            outbox.at[m, q, place], inbox.at[m, q, place], in_recv_sem.at[m, q, place]
        )

    def part_copy(m, q, to, source):
        return remote(
            partial.at[m, q, to],
            returned.at[m, q, source],
            part_send_sem.at[m, q, to],
            ret_recv_sem.at[m, q, source],
            plane * experts + to,
        )

    def part_local(m, q):
        return pltpu.make_async_copy(
            partial.at[m, q, place], returned.at[m, q, place], ret_recv_sem.at[m, q, place]
        )

    def back_copy(m, q, source):
        return remote(
            plane_send.at[m, q],
            plane_back.at[m, source],
            back_send_sem.at[m, q],
            back_recv_sem.at[m, source],
            q * experts + place,
        )

    def placing_of(r, m, q):
        chosen = peer_routes[q, pl.ds(r * micros + m, 1), :][:, :tok]
        onehot = lax.broadcasted_iota(jnp.int32, (experts, tok), 0) == chosen
        earlier = lax.broadcasted_iota(jnp.int32, (tok, tok), 0) < lax.broadcasted_iota(
            jnp.int32, (tok, tok), 1
        )
        counts = jnp.dot(
            onehot.astype(jnp.float32).astype(jnp.bfloat16),
            earlier.astype(jnp.float32).astype(jnp.bfloat16),
            preferred_element_type=jnp.float32,
        )
        slot = jnp.sum(jnp.where(onehot, counts, 0.0), axis=0, keepdims=True).astype(jnp.int32)
        flat = chosen * capacity + slot
        return (lax.broadcasted_iota(jnp.int32, (slots, tok), 0) == flat).astype(jnp.float32)

    def norm_and_send(r, m):
        source = acts_ref if r == 0 else out_ref
        if r > 0:
            passing(m, plane, lambda copy: copy.wait_send())

        def add_squares(c, total):
            x = source[m, :, cols(c)].astype(jnp.float32)
            return total + jnp.sum(x * x, axis=1, keepdims=True)

        squares = lax.fori_loop(0, tiles, add_squares, jnp.zeros((tok, 1), jnp.float32))
        scale = lax.rsqrt(squares / width + 1e-06)

        def scaled(c):
            x = source[m, :, cols(c)].astype(jnp.float32)
            tokens[m, plane, :, cols(c)] = (x * scale * gain_ref[:, cols(c)]).astype(jnp.bfloat16)

        each(0, tiles, scaled)
        passing(m, plane, lambda copy: copy.start())
        scores = jnp.dot(tokens[m, plane], router_ref[...], preferred_element_type=jnp.float32)
        chosen = route_cols_ref[r, m]
        onehot = lax.broadcasted_iota(jnp.int32, (tok, experts), 1) == chosen
        return jax.nn.sigmoid(jnp.sum(jnp.where(onehot, scores, 0.0), axis=1, keepdims=True))

    def pack(r, m, k):
        q = nearest(plane, k, planes)
        if k > 0:
            token_copy(m, q, 1).wait_recv()
            passing(m, q, lambda copy: copy.start())

        if r > 0:
            each(1, experts, lambda d: out_copy(m, q, place_peer(d), place).wait_send())
        placing = placing_of(r, m, q).astype(jnp.bfloat16)

        def packed(c):
            rows = jnp.dot(placing, tokens[m, q, :, cols(c)], preferred_element_type=jnp.float32)
            outbox[m, q, :, :, cols(c)] = rows.astype(jnp.bfloat16).reshape(
                experts, capacity, tile
            )

        each(0, tiles, packed)
        out_local(m, q).start()
        each(1, experts, lambda d: out_copy(m, q, place_peer(d), place).start())

    def expert(r, m, k):
        q = nearest(plane, k, planes)
        out_local(m, q).wait()

        def arrived(d):
            out_copy(m, q, place_peer(d), place_peer(d)).wait_recv()

        each(1, experts, arrived)
        if r > 0:
            each(1, experts, lambda d: part_copy(m, q, place_peer(d), place).wait_send())
        rows = inbox[m, q].reshape(slots, width)
        gate_proj = jnp.dot(rows, gate_ref[...], preferred_element_type=jnp.float32)
        up_proj = jnp.dot(rows, up_ref[...], preferred_element_type=jnp.float32)
        hidden = (jax.nn.silu(gate_proj) * up_proj).astype(jnp.bfloat16)

        def projected(c):
            part = jnp.dot(hidden, down_ref[:, cols(c)], preferred_element_type=jnp.float32)
            partial[m, q, :, :, cols(c)] = part.astype(jnp.bfloat16).reshape(
                experts, capacity, tile
            )

        each(0, tiles, projected)
        part_local(m, q).start()
        each(1, experts, lambda d: part_copy(m, q, place_peer(d), place).start())

    def unpack(r, m, k):
        q = nearest(plane, k, planes)
        part_local(m, q).wait()

        def arrived(d):
            part_copy(m, q, place_peer(d), place_peer(d)).wait_recv()

        each(1, experts, arrived)
        if k > 0:
            passing(m, q, lambda copy: copy.wait_send())
            if r > 0:
                back_copy(m, q, plane).wait_send()

        picking = placing_of(r, m, q).T.astype(jnp.bfloat16)

        def picked(c):
            rows = returned[m, q, :, :, cols(c)].reshape(slots, tile)
            plane_send[m, q, :, cols(c)] = jnp.dot(
                picking, rows, preferred_element_type=jnp.float32
            ).astype(jnp.bfloat16)

        each(0, tiles, picked)

        if k > 0:
            back_copy(m, q, plane).start()

    def finish(r, m, gate_val):
        source = acts_ref if r == 0 else out_ref
        each(1, planes, lambda k: back_copy(m, plane_peer(k), plane_peer(k)).wait_recv())

        def summed(c):
            total = plane_send[m, plane, :, cols(c)].astype(jnp.float32)
            for k in range(1, planes):
                total += plane_back[m, plane_peer(k), :, cols(c)].astype(jnp.float32)
            x = source[m, :, cols(c)].astype(jnp.float32)
            out_ref[m, :, cols(c)] = (x + gate_val * total).astype(jnp.bfloat16)

        each(0, tiles, summed)

    peer_routes[plane] = route_rows_ref[...]
    each(1, planes, lambda k: route_copy(k, plane).start())
    gates = {}
    for kind, r, m, k in order_of_work(rounds, micros, planes):
        if kind == "norm":
            gates[m] = norm_and_send(r, m)
        elif kind == "routes":
            each(1, planes, lambda k: route_copy(k, plane_peer(k)).wait_recv())
        elif kind == "pack":
            pack(r, m, k)
        elif kind == "expert":
            expert(r, m, k)
        elif kind == "unpack":
            unpack(r, m, k)
        else:
            finish(r, m, gates[m])

    each(1, planes, lambda k: route_copy(k, plane).wait_send())
    for m in range(micros):
        passing(m, plane, lambda copy: copy.wait_send())

        def sent(k):
            q = plane_peer(k)
            each(1, experts, lambda d: out_copy(m, q, place_peer(d), place).wait_send())
            each(1, experts, lambda d: part_copy(m, q, place_peer(d), place).wait_send())

            @pl.when(k > 0)
            def _():
                back_copy(m, q, plane).wait_send()

        each(0, planes, sent)


def run_layers(acts, gain, router, routes, gate_mat, up_mat, down_mat):
    devices = lax.axis_size("expert")
    experts = router.shape[1]
    planes = devices // experts
    micros, tok, width = acts.shape
    rounds = routes.shape[0]
    capacity = 2 * tok // experts
    hidden = gate_mat.shape[1]
    rows = rounds * micros
    row_pad, lane_pad = -(-rows // 8) * 8, -(-tok // 128) * 128
    route_rows = jnp.pad(
        routes.reshape(rows, tok), ((0, row_pad - rows), (0, lane_pad - tok))
    )
    vmem = pl.BlockSpec(memory_space=pltpu.VMEM)
    dma = pltpu.SemaphoreType.DMA
    slot_shape = (micros, planes, experts, capacity, width)
    plane_shape = (micros, planes, tok, width)
    slots = experts * capacity
    flops = 2 * rows * planes * slots * width * hidden * 3
    return pl.pallas_call(
        functools.partial(layers_kernel, rounds, micros, planes, experts, capacity),
        out_shape=jax.ShapeDtypeStruct(acts.shape, acts.dtype),
        in_specs=[vmem] * 8,
        out_specs=vmem,
        scratch_shapes=[
            pltpu.VMEM((planes, row_pad, lane_pad), jnp.int32),
            pltpu.VMEM(plane_shape, jnp.bfloat16),
            pltpu.VMEM(slot_shape, jnp.bfloat16),
            pltpu.VMEM(slot_shape, jnp.bfloat16),
            pltpu.VMEM(slot_shape, jnp.bfloat16),
            pltpu.VMEM(slot_shape, jnp.bfloat16),
            pltpu.VMEM(plane_shape, jnp.bfloat16),
            pltpu.VMEM(plane_shape, jnp.bfloat16),
            dma((planes,)),
            dma((planes,)),
            dma((micros, planes + 1)),
            dma((micros, planes)),
            dma((micros, planes, experts)),
            dma((micros, planes, experts)),
            dma((micros, planes, experts)),
            dma((micros, planes, experts)),
            dma((micros, planes)),
            dma((micros, planes)),
        ],
        compiler_params=pltpu.CompilerParams(
            collective_id=0, has_side_effects=True, vmem_limit_bytes=62 * 1024 * 1024
        ),
        cost_estimate=pl.CostEstimate(
            flops=flops,
            bytes_accessed=3 * gate_mat.size * 2 + 4 * acts.size,
            transcendentals=rows * planes * slots * hidden,
        ),
    )(acts, gain, router, route_rows, routes, gate_mat, up_mat, down_mat)


def body(acts, norm_gain, router, routes, w_gate, w_up, w_down):
    sections = lax.axis_size("section")
    rounds = routes.shape[1]
    weights = (w_gate[0, 0], w_up[0, 0], w_down[0, 0])
    if sections == 1:
        return run_layers(acts[0], norm_gain, router[0], routes[0], *weights)[None]
    carried = acts[0]
    pairs = [(source, (source + 1) % sections) for source in range(sections)]
    for r in range(rounds):
        carried = run_layers(carried, norm_gain, router[0], routes[0, r : r + 1], *weights)
        carried = lax.ppermute(carried, "section", pairs)
    return carried[None]


def solution(mesh):
    in_specs = (
        P("section", None, "expert", None),
        P("section", None),
        P("section", None, None),
        P("section", None, None, "expert", None),
        P("section", "expert", None, None),
        P("section", "expert", None, None),
        P("section", "expert", None, None),
    )
    out_specs = P("section", None, "expert", None)
    return jax.shard_map(body, mesh=mesh, in_specs=in_specs, out_specs=out_specs, check_vma=False)
```
